32 devices in a mesh: feat: 8 (over z, y), tok: 4 (over x, core).
Axes of the slice: x: 2, y: 2, z: 4, core: 2. Of those that a mesh axis runs over, the one named last changes fastest.
Arguments:
- activations: bfloat16 [2560, 13312], P('tok', 'feat'), may hold values from -18 to 18
- hessian: float32 [64, 1664, 1664], P('feat', 'tok'), may hold values from -6 to 6
Outputs:
- updated: float32 [64, 1664, 1664], P('feat', 'tok')
The draws below stay inside these ranges and needn't reach their ends.
All inputs are finite; a program needn't handle non-finite values.
Results may differ from the reference program's by a relative error of at most 0.0003.
Values may be sent and summed in bfloat16 or wider, within the bound.
A program may use at most 256 MiB of HBM per device.

```python
import math
import jax
import jax.numpy as jnp
from jax import lax

F = 13312
TILES = 8
TILE = 1664
TOKENS = 2560
SEEN = 5120


def draw_activations(key, part):
    keys = jax.random.split(key, 2)
    scales = jnp.exp(jax.random.uniform(keys[0], (1, F), jnp.float32, math.log(0.3), math.log(3.0)))
    values = jnp.clip(jax.random.normal(keys[1], (TOKENS, F), jnp.float32), -6.0, 6.0) * scales
    return values.astype(jnp.bfloat16)


def levels(stream_key, dims, cuts, low, high):
    def one(dim, blocks):
        steps = jax.random.uniform(jax.random.fold_in(jax.random.fold_in(stream_key, 6), dim), (blocks,), jnp.float32, low / len(cuts), high / len(cuts))
        return jnp.repeat(jnp.exp(steps), dims[dim] // blocks).reshape((-1,) + (1,) * (len(dims) - dim - 1))

    loudness = one(*cuts[0])
    for cut in cuts[1:]:
        loudness = loudness * one(*cut)
    return loudness


def gaussian(own_key, dims, deviation, most, cuts=(), kind=jnp.bfloat16):
    loudness = levels(own_key, dims, cuts, -0.22, 0.18) if cuts else 1.0
    values = jax.random.normal(own_key, dims, jnp.float32) * deviation * loudness
    return jnp.minimum(jnp.maximum(values, -most), most).astype(kind)


def setup_inputs(seed: int = 0) -> dict:
    key_of = jax.random.split(jax.random.key(seed), 3)
    return {
        "activations": draw_activations(jax.random.fold_in(key_of[2], 71), 0),
        "hessian": gaussian(key_of[1], (TILES * TILES, TILE, TILE), 1.0, 6.0, ((0, 8), (1, 4)), jnp.float32),
    }


def reference(activations, hessian):
    values = activations.astype(jnp.float32)
    seen_share = SEEN / (SEEN + TOKENS)
    weight_new = 2.0 / (SEEN + TOKENS)

    def one_tile(tile_index):
        row_tile = tile_index // TILES
        col_tile = tile_index % TILES
        row_block = lax.dynamic_slice_in_dim(values, row_tile * TILE, TILE, 1)
        col_block = lax.dynamic_slice_in_dim(values, col_tile * TILE, TILE, 1)
        sums = lax.cond(
            row_tile >= col_tile,
            lambda: jnp.dot(col_block.T, row_block, precision=lax.Precision.HIGHEST, preferred_element_type=values.dtype),
            lambda: jnp.zeros((TILE, TILE), values.dtype),
        )
        row_ids = row_tile * TILE + jnp.arange(TILE, dtype=jnp.int32)
        col_ids = col_tile * TILE + jnp.arange(TILE, dtype=jnp.int32)
        lower = row_ids[None, :] >= col_ids[:, None]
        previous = hessian[tile_index]
        return jnp.where(lower, seen_share * previous + weight_new * sums, previous)

    return lax.map(one_tile, jnp.arange(TILES * TILES, dtype=jnp.int32))
```

```python
import jax
import jax.numpy as jnp
from jax import lax
from jax.experimental import pallas as pl
from jax.experimental.pallas import tpu as pltpu
from jax.sharding import PartitionSpec as P

TILES = 8
MESH = pl.DeviceIdType.MESH


def contract_tokens(left, right):
    return lax.dot_general(
        left, right, (((0,), (0,)), ((), ())), preferred_element_type=jnp.float32
    )


def tile_sums(row_block, col_block, lower_tile):
    width = row_block.shape[1]
    quarter_width = col_block.shape[1] // lax.axis_size("tok")
    every_rows = lax.all_gather(row_block, "tok", axis=0, tiled=True)
    every_cols = lax.all_to_all(col_block, "tok", split_axis=1, concat_axis=0, tiled=True)
    return lax.cond(
        lower_tile,
        lambda: contract_tokens(every_cols, every_rows),
        lambda: jnp.zeros((quarter_width, width), jnp.float32),
    )


def shares(activations):
    total_tokens = activations.shape[0] * lax.axis_size("tok")
    seen_tokens = 2 * total_tokens
    return seen_tokens / (seen_tokens + total_tokens), 2.0 / (seen_tokens + total_tokens)


def on_device_general(activations, hessian):
    seen_share, weight_new = shares(activations)
    position = lax.axis_index("feat")
    tok_position = lax.axis_index("tok")
    local_tiles = hessian.shape[0]
    quarter_width = hessian.shape[1]
    width = hessian.shape[2]
    gathered = lax.all_gather(activations, "feat", axis=1, tiled=True)
    results = []
    for slot in range(local_tiles):
        tile_index = position * local_tiles + slot
        row_tile = tile_index // TILES
        col_tile = tile_index % TILES
        row_block = lax.dynamic_slice_in_dim(gathered, row_tile * width, width, 1)
        col_block = lax.dynamic_slice_in_dim(gathered, col_tile * width, width, 1)
        sums = tile_sums(row_block, col_block, row_tile >= col_tile)
        row_ids = row_tile * width + jnp.arange(width, dtype=jnp.int32)
        col_ids = (
            col_tile * width
            + tok_position * quarter_width
            + jnp.arange(quarter_width, dtype=jnp.int32)
        )
        lower = row_ids[None, :] >= col_ids[:, None]
        previous = hessian[slot]
        results.append(jnp.where(lower, seen_share * previous + weight_new * sums, previous))
    return jnp.stack(results)


def share_kernel(feat, tok, a_ref, at_ref, cols, rows, up_sem, side_sem, swap_sem, in_sem,
                 row_send, row_in, local_sem):
    p = lax.axis_index("feat")
    t = lax.axis_index("tok")
    y = p % 2
    z = p // 2
    last_z = feat // 2 - 1
    up = p + 2
    side = p + 1 - 2 * y
    near = [t, t + 1 - 2 * (t % 2), (t + 2) % 4, 3 - t]
    tokens, width = a_ref.shape
    quarter = width // tok
    has_up = z < last_z

    barrier = pltpu.get_barrier_semaphore()
    for r in (1, 2, 3):
        pl.semaphore_signal(barrier, inc=1, device_id=(p, near[r]), device_id_type=MESH)
    pl.semaphore_signal(barrier, inc=1, device_id=(side, t), device_id_type=MESH)

    @pl.when(has_up)
    def _():
        pl.semaphore_signal(barrier, inc=1, device_id=(up, t), device_id_type=MESH)

    @pl.when(z > 0)
    def _():
        pl.semaphore_signal(barrier, inc=1, device_id=(p - 2, t), device_id_type=MESH)

    pl.semaphore_wait(barrier, 4 + has_up.astype(jnp.int32) + (z > 0).astype(jnp.int32))

    def block(j, who):
        return cols.at[j, :, pl.ds(pl.multiple_of(who * tokens, tokens), tokens)]

    def mine(who):
        return at_ref.at[pl.ds(pl.multiple_of(who * quarter, quarter), quarter), :]

    def row_block(who):
        return rows.at[pl.ds(pl.multiple_of(who * tokens, tokens), tokens), :]

    def move(src, j, who, send, device):
        return pltpu.make_async_remote_copy(
            src_ref=src, dst_ref=block(j, who), send_sem=send, recv_sem=in_sem.at[j, who],
            device_id=device, device_id_type=MESH)

    def arrive(j, r):
        move(block(j, near[r]), j, near[r], up_sem.at[j, r], (side, t)).wait_recv()

    def send_row(src, who, index, device):
        return pltpu.make_async_remote_copy(
            src_ref=src, dst_ref=row_block(who), send_sem=row_send.at[index],
            recv_sem=row_in.at[who], device_id=device, device_id_type=MESH)

    ended = []

    def start_if(cond, copy):
        @pl.when(cond)
        def _():
            copy.start()
        ended.append((cond, copy))

    def lane(even, r, j):
        if even:
            return r % 2 + 0 * j
        return jnp.where((r == 3) | ((r == 2) & (j == feat - 3)), 0, 1)

    def forward_up(j, r, lane_of, src=None):
        src = block(j, near[r]) if src is None else src
        start_if(has_up & (lane_of == y), move(src, j, near[r], up_sem.at[j, r], (up, t)))

    swaps = [move(mine(near[r]), p, t, swap_sem.at[r], (p, near[r])) for r in (2, 3, 1)]
    for copy in swaps:
        copy.start()
    own_cols = pltpu.make_async_copy(mine(t), block(p, t), local_sem.at[0])
    own_rows = pltpu.make_async_copy(a_ref, row_block(t), local_sem.at[1])
    own_lane = [jnp.where(y == 0, r % 2, lane(False, r, p)) for r in range(4)]
    side_lane = [jnp.where(y == 1, r % 2, lane(False, r, side)) for r in range(4)]
    row_sends = [send_row(a_ref, t, 0, (p, near[2])), send_row(a_ref, t, 1, (p, near[1]))]

    for r in range(4):
        if r:
            arrive(p, r)
        src = mine(t) if r == 0 else None
        forward_up(p, r, own_lane[r], src)
        start_if((y == 0) | (has_up & (own_lane[r] == 0)),
                 move(block(p, near[r]) if src is None else src, p, near[r],
                      side_sem.at[p, r], (side, t)))
        if r == 0:
            own_cols.start()
            own_rows.start()
        if r == 1:
            for copy in row_sends:
                copy.start()

    for r in range(4):
        @pl.when((y == 1) | (has_up & (side_lane[r] == 0)))
        def _():
            arrive(side, r)
        forward_up(side, r, side_lane[r])

    pass_row = send_row(row_block(near[2]), near[2], 2, (p, near[1]))

    def pass_rows():
        send_row(row_block(near[2]), near[2], 2, (p, near[2])).wait_recv()
        pass_row.start()

    own_rows.wait()
    for dz in range(1, last_z + 1):
        for even in (True, False):
            for r in range(4):
                j = jnp.maximum(2 * (z - dz) + (0 if even else 1), 0)
                here = lane(even, r, j) == y
                cond = (z >= dz) & here

                @pl.when(cond)
                def _():
                    arrive(j, r)
                start_if(cond & has_up, move(block(j, near[r]), j, near[r], up_sem.at[j, r], (up, t)))
                start_if(cond, move(block(j, near[r]), j, near[r], side_sem.at[j, r], (side, t)))
        if dz == 1:
            pass_rows()

    for dz in range(1, last_z + 1):
        for even in (True, False):
            for r in range(4):
                j = jnp.maximum(2 * (z - dz) + (0 if even else 1), 0)

                @pl.when((z >= dz) & (lane(even, r, j) != y))
                def _():
                    arrive(j, r)

    for r in (1, 3):
        send_row(row_block(near[r]), near[r], 2, (p, near[1])).wait_recv()
    own_cols.wait()
    for copy in swaps + row_sends + [pass_row]:
        copy.wait_send()
    for cond, copy in ended:
        @pl.when(cond)
        def _():
            copy.wait_send()


def blend_kernel(seen_share, weight_new, pos, cols, rows, h, out):
    j = pl.program_id(0)
    width = rows.shape[1]
    quarter = h.shape[1]

    def part(start, size):
        at = pl.ds(start, size)
        sums = jnp.dot(cols[0], rows[:, at], preferred_element_type=jnp.float32)
        old = h[0, :, at]
        row_ids = pos[0] * width + start + lax.broadcasted_iota(jnp.int32, (1, size), 1)
        col_ids = j * width + pos[1] * quarter + lax.broadcasted_iota(jnp.int32, (quarter, 1), 0)
        out[0, :, at] = jnp.where(row_ids >= col_ids, seen_share * old + weight_new * sums, old)

    @pl.when(j <= pos[0])
    def _():
        step = 256
        @pl.loop(0, width // step)
        def _(i):
            part(pl.multiple_of(i * step, step), step)
        if width % step:
            part(width // step * step, width % step)

    @pl.when(j > pos[0])
    def _():
        out[...] = h[...]


def on_device_panels(activations, hessian):
    feat, tok = lax.axis_size("feat"), lax.axis_size("tok")
    tokens, width = activations.shape
    tiles, quarter, _ = hessian.shape
    any_space = pl.BlockSpec(memory_space=pl.ANY)
    dma = pltpu.SemaphoreType.DMA
    cols, rows = pl.pallas_call(
        lambda *refs: share_kernel(feat, tok, *refs),
        out_shape=(
            jax.ShapeDtypeStruct((feat, quarter, tok * tokens), activations.dtype),
            jax.ShapeDtypeStruct((tok * tokens, width), activations.dtype),
        ),
        in_specs=[any_space] * 2,
        out_specs=(any_space, any_space),
        scratch_shapes=[dma((feat, tok)), dma((feat, tok)), dma((tok,)), dma((feat, tok)),
                        dma((3,)), dma((tok,)), dma((2,))],
        compiler_params=pltpu.CompilerParams(collective_id=0, has_side_effects=True),
        name="share",
    )(activations, activations.T)
    seen_share, weight_new = shares(activations)
    pos = jnp.stack([lax.axis_index("feat"), lax.axis_index("tok")]).astype(jnp.int32)
    tile = pl.BlockSpec((1, quarter, width), lambda j, pos: (j, 0, 0))
    return pl.pallas_call(
        lambda *refs: blend_kernel(seen_share, weight_new, *refs),
        out_shape=jax.ShapeDtypeStruct(hessian.shape, hessian.dtype),
        grid_spec=pltpu.PrefetchScalarGridSpec(
            num_scalar_prefetch=1,
            grid=(tiles,),
            in_specs=[
                pl.BlockSpec((1, quarter, tok * tokens),
                             lambda j, pos: (jnp.minimum(j, pos[0]), 0, 0)),
                pl.BlockSpec((tok * tokens, width), lambda j, pos: (0, 0),
                             pipeline_mode=pl.Buffered(1)),
                tile,
            ],
            out_specs=tile,
        ),
        compiler_params=pltpu.CompilerParams(vmem_limit_bytes=48 * 1024 * 1024),
        name="blend",
    )(pos, cols, rows, hessian)


def on_device(activations, hessian):
    tokens, width = activations.shape
    whole_panels = (
        lax.axis_size("feat") == TILES
        and lax.axis_size("tok") == 4
        and hessian.shape[0] == TILES
        and hessian.shape[2] == width
        and width % 128 == 0
        and hessian.shape[1] % 16 == 0
        and tokens % 128 == 0
    )
    return (on_device_panels if whole_panels else on_device_general)(activations, hessian)


def solution(mesh):
    in_specs = (P("tok", "feat"), P("feat", "tok", None))
    out_specs = P("feat", "tok", None)
    return jax.shard_map(
        on_device, mesh=mesh, in_specs=in_specs, out_specs=out_specs, check_vma=False
    )
```

```python
import jax
import jax.numpy as jnp
from jax import lax
from jax.experimental import pallas as pl
from jax.experimental.pallas import tpu as pltpu
from jax.sharding import PartitionSpec as P

TILES = 8
MESH = pl.DeviceIdType.MESH


def contract_tokens(left, right):
    return lax.dot_general(
        left, right, (((0,), (0,)), ((), ())), preferred_element_type=jnp.float32
    )


def tile_sums(row_block, col_block, lower_tile):
    width = row_block.shape[1]
    quarter_width = col_block.shape[1] // lax.axis_size("tok")
    every_rows = lax.all_gather(row_block, "tok", axis=0, tiled=True)
    every_cols = lax.all_to_all(col_block, "tok", split_axis=1, concat_axis=0, tiled=True)
    return lax.cond(
        lower_tile,
        lambda: contract_tokens(every_cols, every_rows),
        lambda: jnp.zeros((quarter_width, width), jnp.float32),
    )


def shares(activations):
    total_tokens = activations.shape[0] * lax.axis_size("tok")
    seen_tokens = 2 * total_tokens
    return seen_tokens / (seen_tokens + total_tokens), 2.0 / (seen_tokens + total_tokens)


def on_device_general(activations, hessian):
    seen_share, weight_new = shares(activations)
    position = lax.axis_index("feat")
    tok_position = lax.axis_index("tok")
    local_tiles = hessian.shape[0]
    quarter_width = hessian.shape[1]
    width = hessian.shape[2]
    gathered = lax.all_gather(activations, "feat", axis=1, tiled=True)
    results = []
    for slot in range(local_tiles):
        tile_index = position * local_tiles + slot
        row_tile = tile_index // TILES
        col_tile = tile_index % TILES
        row_block = lax.dynamic_slice_in_dim(gathered, row_tile * width, width, 1)
        col_block = lax.dynamic_slice_in_dim(gathered, col_tile * width, width, 1)
        sums = tile_sums(row_block, col_block, row_tile >= col_tile)
        row_ids = row_tile * width + jnp.arange(width, dtype=jnp.int32)
        col_ids = (
            col_tile * width
            + tok_position * quarter_width
            + jnp.arange(quarter_width, dtype=jnp.int32)
        )
        lower = row_ids[None, :] >= col_ids[:, None]
        previous = hessian[slot]
        results.append(jnp.where(lower, seen_share * previous + weight_new * sums, previous))
    return jnp.stack(results)


def share_kernel(feat, tok, a_ref, at_ref, cols, rows, up_sem, side_sem, swap_sem, in_sem,
                 row_send, row_in, local_sem):
    p = lax.axis_index("feat")
    t = lax.axis_index("tok")
    y = p % 2
    z = p // 2
    last_z = feat // 2 - 1
    up = p + 2
    side = p + 1 - 2 * y
    near = [t, t + 1 - 2 * (t % 2), (t + 2) % 4, 3 - t]
    tokens, width = a_ref.shape
    quarter = width // tok
    has_up = z < last_z

    barrier = pltpu.get_barrier_semaphore()
    for r in (1, 2, 3):
        pl.semaphore_signal(barrier, inc=1, device_id=(p, near[r]), device_id_type=MESH)
    pl.semaphore_signal(barrier, inc=1, device_id=(side, t), device_id_type=MESH)

    @pl.when(has_up)
    def _():
        pl.semaphore_signal(barrier, inc=1, device_id=(up, t), device_id_type=MESH)

    @pl.when(z > 0)
    def _():
        pl.semaphore_signal(barrier, inc=1, device_id=(p - 2, t), device_id_type=MESH)

    pl.semaphore_wait(barrier, 4 + has_up.astype(jnp.int32) + (z > 0).astype(jnp.int32))

    def block(j, who):
        return cols.at[j, :, pl.ds(pl.multiple_of(who * tokens, tokens), tokens)]

    def mine(who):
        return at_ref.at[pl.ds(pl.multiple_of(who * quarter, quarter), quarter), :]

    def row_block(who):
        return rows.at[pl.ds(pl.multiple_of(who * tokens, tokens), tokens), :]

    def move(src, j, who, send, device):
        return pltpu.make_async_remote_copy(
            src_ref=src, dst_ref=block(j, who), send_sem=send, recv_sem=in_sem.at[j, who],
            device_id=device, device_id_type=MESH)

    def arrive(j, r):
        move(block(j, near[r]), j, near[r], up_sem.at[j, r], (side, t)).wait_recv()

    def send_row(src, who, index, device):
        return pltpu.make_async_remote_copy(
            src_ref=src, dst_ref=row_block(who), send_sem=row_send.at[index],
            recv_sem=row_in.at[who], device_id=device, device_id_type=MESH)

    ended = []

    def start_if(cond, copy):
        @pl.when(cond)
        def _():
            copy.start()
        ended.append((cond, copy))

    def lane(r, j):
        odd_lane = jnp.where((r == 3) | ((r == 2) & (j > 1)), 0, 1)
        return jnp.where(j % 2 == 0, r % 2, odd_lane)

    def forward_up(j, r, lane_of, src=None):
        src = block(j, near[r]) if src is None else src
        start_if(has_up & (lane_of == y), move(src, j, near[r], up_sem.at[j, r], (up, t)))

    swaps = [move(mine(near[r]), p, t, swap_sem.at[r], (p, near[r])) for r in (2, 3, 1)]
    for copy in swaps:
        copy.start()
    own_cols = pltpu.make_async_copy(mine(t), block(p, t), local_sem.at[0])
    own_rows = pltpu.make_async_copy(a_ref, row_block(t), local_sem.at[1])
    row_sends = [send_row(a_ref, t, 0, (p, near[2])), send_row(a_ref, t, 1, (p, near[1]))]

    def own_block(r):
        if r:
            arrive(p, r)
        src = mine(t) if r == 0 else block(p, near[r])
        forward_up(p, r, lane(r, p), src)
        start_if((y == 0) | (has_up & (lane(r, p) == 0)),
                 move(src, p, near[r], side_sem.at[p, r], (side, t)))

    def side_block(r):
        @pl.when(has_up & ((y == 1) | (lane(r, side) == 0)))
        def _():
            arrive(side, r)
        forward_up(side, r, lane(r, side))

    def pass_block(dz, first, r):
        j = jnp.maximum(2 * (z - dz) + (y if first else 1 - y), 0)
        cond = (z >= dz) & (lane(r, j) == y)

        @pl.when(cond)
        def _():
            arrive(j, r)
        start_if(cond & has_up, move(block(j, near[r]), j, near[r], up_sem.at[j, r], (up, t)))
        start_if(cond, move(block(j, near[r]), j, near[r], side_sem.at[j, r], (side, t)))

    own_block(0)
    own_cols.start()
    own_rows.start()
    first_cond, first_copy = ended.pop(0)

    @pl.when(first_cond)
    def _():
        first_copy.wait_send()

    own_block(1)
    side_block(0)
    side_block(1)
    pass_block(1, True, 0)
    pass_block(1, True, 1)
    own_block(2)
    own_block(3)
    for copy in row_sends:
        copy.start()
    side_block(2)
    side_block(3)

    pass_row = send_row(row_block(near[2]), near[2], 2, (p, near[1]))

    def pass_rows():
        send_row(row_block(near[2]), near[2], 2, (p, near[2])).wait_recv()
        pass_row.start()

    own_rows.wait()
    for dz in range(1, last_z + 1):
        for first in (True, False):
            for r in range(4):
                if (dz, first, r) not in ((1, True, 0), (1, True, 1)):
                    pass_block(dz, first, r)
        if dz == max(last_z - 1, 1):
            pass_rows()

    for dz in range(1, last_z + 1):
        for k in (0, 1):
            for r in range(4):
                j = jnp.maximum(2 * (z - dz) + k, 0)

                @pl.when((z >= dz) & (lane(r, j) != y))
                def _():
                    arrive(j, r)

    for r in range(4):
        @pl.when((z == last_z) & (y == 1))
        def _():
            arrive(side, r)

    for r in (1, 3):
        send_row(row_block(near[r]), near[r], 2, (p, near[1])).wait_recv()
    own_cols.wait()
    for copy in swaps + row_sends + [pass_row]:
        copy.wait_send()
    for cond, copy in ended:
        @pl.when(cond)
        def _():
            copy.wait_send()


def blend_kernel(seen_share, weight_new, pos, cols, rows, h, out):
    j = pl.program_id(0)
    width = rows.shape[1]
    quarter = h.shape[1]

    def part(start, size):
        at = pl.ds(start, size)
        sums = jnp.dot(cols[0], rows[:, at], preferred_element_type=jnp.float32)
        old = h[0, :, at]
        row_ids = pos[0] * width + start + lax.broadcasted_iota(jnp.int32, (1, size), 1)
        col_ids = j * width + pos[1] * quarter + lax.broadcasted_iota(jnp.int32, (quarter, 1), 0)
        out[0, :, at] = jnp.where(row_ids >= col_ids, seen_share * old + weight_new * sums, old)

    @pl.when(j <= pos[0])
    def _():
        step = 256
        for start in range(0, width, step):
            part(start, min(step, width - start))

    @pl.when(j > pos[0])
    def _():
        out[...] = h[...]


def on_device_panels(activations, hessian):
    feat, tok = lax.axis_size("feat"), lax.axis_size("tok")
    tokens, width = activations.shape
    tiles, quarter, _ = hessian.shape
    any_space = pl.BlockSpec(memory_space=pl.ANY)
    dma = pltpu.SemaphoreType.DMA
    cols, rows = pl.pallas_call(
        lambda *refs: share_kernel(feat, tok, *refs),
        out_shape=(
            jax.ShapeDtypeStruct((feat, quarter, tok * tokens), activations.dtype),
            jax.ShapeDtypeStruct((tok * tokens, width), activations.dtype),
        ),
        in_specs=[any_space] * 2,
        out_specs=(any_space, any_space),
        scratch_shapes=[dma((feat, tok)), dma((feat, tok)), dma((tok,)), dma((feat, tok)),
                        dma((3,)), dma((tok,)), dma((2,))],
        compiler_params=pltpu.CompilerParams(collective_id=0, has_side_effects=True),
        name="share",
    )(activations, activations.T)
    seen_share, weight_new = shares(activations)
    pos = jnp.stack([lax.axis_index("feat"), lax.axis_index("tok")]).astype(jnp.int32)
    tile = pl.BlockSpec((1, quarter, width), lambda j, pos: (j, 0, 0))
    return pl.pallas_call(
        lambda *refs: blend_kernel(seen_share, weight_new, *refs),
        out_shape=jax.ShapeDtypeStruct(hessian.shape, hessian.dtype),
        grid_spec=pltpu.PrefetchScalarGridSpec(
            num_scalar_prefetch=1,
            grid=(tiles,),
            in_specs=[
                pl.BlockSpec((1, quarter, tok * tokens),
                             lambda j, pos: (jnp.minimum(j, pos[0]), 0, 0)),
                pl.BlockSpec((tok * tokens, width), lambda j, pos: (0, 0),
                             pipeline_mode=pl.Buffered(1)),
                tile,
            ],
            out_specs=tile,
        ),
        compiler_params=pltpu.CompilerParams(vmem_limit_bytes=48 * 1024 * 1024),
        name="blend",
    )(pos, cols, rows, hessian)


def on_device(activations, hessian):
    tokens, width = activations.shape
    whole_panels = (
        lax.axis_size("feat") == TILES
        and lax.axis_size("tok") == 4
        and hessian.shape[0] == TILES
        and hessian.shape[2] == width
        and width % 128 == 0
        and hessian.shape[1] % 16 == 0
        and tokens % 128 == 0
    )
    return (on_device_panels if whole_panels else on_device_general)(activations, hessian)


def solution(mesh):
    in_specs = (P("tok", "feat"), P("feat", "tok", None))
    out_specs = P("feat", "tok", None)
    return jax.shard_map(
        on_device, mesh=mesh, in_specs=in_specs, out_specs=out_specs, check_vma=False
    )
```
